32 devices in a mesh: groups: 2 (over x), kel: 16 (over z, y, core).
Axes of the slice: x: 2, y: 2, z: 4, core: 2. Of those that a mesh axis runs over, the one named last changes fastest.
Arguments:
- electrons: float32 [32, 8, 64], P(('groups', 'kel')), parts along dimension 0, may hold values from 0 to 1
- phonons: float32 [64, 6, 64], P(('groups', 'kel')), parts along dimension 0, may hold values from 0 to 2
- elec_wannier: bfloat16 [32, 256, 64], P(('groups', 'kel')), parts along dimension 0, may hold values from -6 to 6
- phon_wannier: bfloat16 [64, 256, 64], P(('groups', 'kel')), parts along dimension 0, may hold values from -0.375 to 0.375
- coupling: bfloat16 [48, 256, 256], replicated, may hold values from -0.375 to 0.375
- pair_blocks: int32 [32, 12], P(('groups', 'kel')), parts along dimension 0, may hold values from 0 to 31, as said below
- pair_counts: int32 [32], P(('groups', 'kel')), parts along dimension 0, may hold values from 1 to 12, as said below
- drift_speed: float32 [16], P('groups'), parts along dimension 0, may hold values from 0.2 to 0.8
Outputs:
- electrons_out: float32 [32, 8, 64], P(('groups', 'kel')), parts along dimension 0
- phonons_out: float32 [64, 6, 64], P(('groups', 'kel')), parts along dimension 0
The draws below stay inside these ranges and needn't reach their ends.
There are 2 independent parts, one for each index of `groups`. The reference program is written for one: setup_inputs(seed, part) draws one part's arguments, and reference() takes and returns one part's arrays. A program takes and returns all parts, laid end to end along the dimension named above; an argument that names none is the same for every part. Nothing has to cross between parts.
Inputs may be any that keep to these rules, and one draw needn't show every extreme that they name: `pair_blocks`: within one kx plane the 12 q-blocks are distinct. `pair_counts`: some kx plane has all 12 slots live.
All inputs are finite; a program needn't handle non-finite values.
Results may differ from the reference program's by a relative error of at most 0.0015.
Values may be sent and summed in bfloat16 or wider, within the bound.
A program may use at most 64 MiB of HBM per device.

```python
import math
import jax
import jax.numpy as jnp
from jax import lax

NB = 8
NM = 6
WS = 256
KPB = 64
QPB = 64
PMAX = 12
STEPS = 2
NKX = 16
NQB = 32


def draw_pair_blocks(key, part):
    key = jax.random.fold_in(key, 11)
    keys = jax.random.split(key, NKX)
    rows = jax.vmap(lambda one: jax.random.permutation(one, NQB)[:PMAX])(keys)
    return rows.astype(jnp.int32)


def draw_pair_counts(key, part):
    key = jax.random.fold_in(key, 23)
    first, second = jax.random.split(key)
    counts = jax.random.randint(first, (NKX,), 1, PMAX + 1)
    where_full = jax.random.randint(second, (), 0, NKX)
    return counts.at[where_full].set(PMAX).astype(jnp.int32)


def levels(rng, shape, cuts, smallest, top_value):
    factor_of = 1.0
    for position, parts in cuts:
        heights = jax.random.uniform(jax.random.fold_in(jax.random.fold_in(rng, 6), position), (parts,), jnp.float32, smallest / len(cuts), top_value / len(cuts))
        factor_of = factor_of * jnp.repeat(jnp.exp(heights), shape[position] // parts).reshape((-1,) + (1,) * (len(shape) - 1 - position))
    return factor_of


def normal_values(rng, dims, width, bound, pieces=(), held_as=jnp.bfloat16):
    values = width * jax.random.normal(rng, dims, jnp.float32)
    if pieces:
        values = values * levels(rng, dims, pieces, -0.22, 0.18)
    return jnp.clip(values, -bound, bound).astype(held_as)


def setup_inputs(seed: int = 0, part: int = 0) -> dict:
    arg_keys = jax.random.split(jax.random.key(seed), 9)
    part_keys = jax.random.split(jax.random.fold_in(arg_keys[8], part), 9)
    return {
        "electrons": jnp.clip(1.0 * jax.random.uniform(part_keys[0], (NKX, NB, KPB), jnp.float32) ** levels(part_keys[0], (NKX, NB, KPB), ((0, 16),), -0.2, 0.2), 0.0, 1.0),
        "phonons": jnp.clip(2.0 * jax.random.uniform(part_keys[1], (NQB, NM, QPB), jnp.float32) ** levels(part_keys[1], (NQB, NM, QPB), ((0, 16),), -0.2, 0.2), 0.0, 2.0),
        "elec_wannier": normal_values(part_keys[2], (NKX, WS, KPB), 1.0, 6.0, ((0, 16),)),
        "phon_wannier": normal_values(part_keys[3], (NQB, WS, QPB), WS ** -0.5, 0.375, ((0, 16),)),
        "coupling": normal_values(arg_keys[4], (NB * NM, WS, WS), WS ** -0.5, 0.375),
        "pair_blocks": draw_pair_blocks(jax.random.fold_in(jax.random.fold_in(arg_keys[8], part), 71), part),
        "pair_counts": draw_pair_counts(jax.random.fold_in(jax.random.fold_in(arg_keys[8], part), 71), part),
        "drift_speed": jnp.clip(jnp.exp(jax.random.uniform(part_keys[7], (NB,), jnp.float32, math.log(0.2), math.log(0.8))), 0.2, 0.8),
    }


step_length = 0.5


def reference(electrons, phonons, elec_wannier, phon_wannier, coupling, pair_blocks, pair_counts, drift_speed):
    hp = lax.Precision.HIGHEST
    coup = coupling.astype(jnp.float32)

    def plane_coupling(x):
        amp = jnp.einsum("ri,crs->cis", elec_wannier[x].astype(jnp.float32), coup).astype(jnp.bfloat16)
        feats = phon_wannier[pair_blocks[x]].astype(jnp.float32)
        field = jnp.einsum("cis,psj->pcij", amp.astype(jnp.float32), feats)
        valid = jnp.arange(PMAX) < pair_counts[x]
        return jnp.where(valid[:, None, None, None], field * field, 0.0).astype(jnp.bfloat16)

    strength = lax.map(plane_coupling, jnp.arange(NKX))

    def rates(occ_e, occ_n):
        def plane_rates(x):
            table = strength[x].astype(jnp.float32).reshape(PMAX, NB, NM, KPB, QPB)
            chosen = occ_n[pair_blocks[x]]
            upper = jnp.einsum("pbmij,pmj->bi", table, 1.0 + 2.0 * chosen, precision=hp)
            lower = jnp.einsum("pbmij,pmj->bi", table, chosen, precision=hp)
            toward = jnp.einsum("pbmij,bi->pmj", table, occ_e[x], precision=hp)
            plain = jnp.sum(table, axis=(1, 3))
            return occ_e[x] * upper - lower, (1.0 + 2.0 * chosen) * toward - chosen * plain

        loss, gained = lax.map(plane_rates, jnp.arange(NKX))
        dense = jnp.zeros((NQB, NM, QPB), jnp.float32).at[pair_blocks.reshape(-1)].add(gained.reshape(-1, NM, QPB))
        previous = jnp.roll(occ_e, 1, axis=0)
        rate_e = -loss / (PMAX * NM * QPB) - drift_speed[None, :, None] * (occ_e - previous)
        rate_n = dense / (PMAX * NB * KPB)
        return rate_e, rate_n

    occ_e, occ_n = electrons, phonons
    for step in range(STEPS):
        first_e, first_n = rates(occ_e, occ_n)
        second_e, second_n = rates(occ_e + step_length * first_e, occ_n + step_length * first_n)
        occ_e = occ_e + 0.5 * step_length * (first_e + second_e)
        occ_n = occ_n + 0.5 * step_length * (first_n + second_n)
    return occ_e, occ_n
```

```python
import functools
import jax
import jax.numpy as jnp
from jax import lax
from jax.experimental import pallas as pl
from jax.experimental.pallas import tpu as pltpu
from jax.sharding import PartitionSpec as P

STEPS = 2
HALF = 0.25
FULL = 0.5
MESH = pl.DeviceIdType.MESH
f32 = jnp.float32
bf16 = jnp.bfloat16


def iota(shape, dim):
    return lax.broadcasted_iota(jnp.int32, shape, dim)


def kernel(
    n, bands, modes, kp, qp, slots, ws,
    elec, phon, ew, pw, coup, ids, counts, speed,
    elec_out, phon_out,
    coup_v, amp, table, feats, init, chosen, msgs, rims,
    rows_s, lanes_s, plain_s, toward_s, nbase, nk1, fbase, fk1, fnow, onehot,
    csem, fsend, frecv, isend, irecv, msend, mrecv, rsend, rrecv,
):
    me = lax.axis_index("kel")
    nbi = bands * kp
    npj = slots * qp
    nmj = modes * qp
    width = init.shape[2]
    bits = n.bit_length() - 1

    def load_coupling(b):
        span = pl.ds(b * modes, modes)
        return pltpu.make_async_copy(coup.at[span], coup_v.at[span], csem.at[b])

    for b in range(bands):
        load_coupling(b).start()

    feats[me] = jnp.concatenate([pw[0], pw[1]], axis=1)
    own = jnp.zeros((8, width), f32)
    rows = iota((8, width), 0)
    lanes = iota((8, width), 1)
    for p in range(slots):
        own = jnp.where((rows == 2) & (lanes == me * 16 + p), (ids[0, p] + 1).astype(f32), own)
    init[me] = own
    for q in range(2):
        for m in range(modes):
            init[me, q : q + 1, m * qp : (m + 1) * qp] = phon[q, m : m + 1, :]
    for b in range(bands):
        init[me, 3:4, b * kp : (b + 1) * kp] = elec[0, b : b + 1, :]

    barrier = pltpu.get_barrier_semaphore()

    def greet(k, _):
        pl.semaphore_signal(
            barrier, inc=1, device_id={"kel": lax.rem(me + k, n)}, device_id_type=MESH
        )
        return 0

    lax.fori_loop(1, n, greet, 0)
    pl.semaphore_wait(barrier, n - 1)

    def partner(bit):
        step = 1 << bit
        return me + step * (1 - 2 * lax.rem(me // step, 2))

    def sends(level):
        bit = bits - 1 - level
        low = 1 << (bit + 1)
        base = lax.rem(me, low)
        return [base + low * t for t in range(1 << level)], partner(bit)

    def ring_copy(ref, ssem, rsem, block, sem, dst):
        return pltpu.make_async_remote_copy(
            src_ref=ref.at[block], dst_ref=ref.at[block],
            send_sem=ssem.at[sem], recv_sem=rsem.at[block],
            device_id={"kel": dst}, device_id_type=MESH)

    def start_level(level):
        blocks, dst = sends(level)
        for t, block in enumerate(blocks):
            sem = (1 << level) - 1 + t
            ring_copy(feats, fsend, frecv, block, sem, dst).start()
            ring_copy(init, isend, irecv, block, sem, dst).start()

    def wait_level(level):
        bit = bits - 1 - level
        low = 1 << (bit + 1)
        dst = partner(bit)
        base = lax.rem(dst, low)
        for t in range(1 << level):
            ring_copy(feats, fsend, frecv, base + low * t, 0, dst).wait_recv()
            ring_copy(init, isend, irecv, base + low * t, 0, dst).wait_recv()

    start_level(0)

    ewt = jnp.transpose(ew[0].astype(f32)).astype(bf16)

    def amps(b, _):
        load_coupling(b).wait()
        for m in range(modes):
            a = jnp.dot(ewt, coup_v[b * modes + m], preferred_element_type=f32)
            amp[m, pl.ds(pl.multiple_of(b * kp, kp), kp), :] = a.astype(bf16)
        return 0

    share = -(-bands // bits)
    done = 0
    for level in range(bits):
        stop = min(bands, done + share)
        lax.fori_loop(done, stop, amps, 0)
        done = stop
        wait_level(level)
        if level + 1 < bits:
            start_level(level + 1)
    for level in range(bits):
        blocks, dst = sends(level)
        for t, block in enumerate(blocks):
            sem = (1 << level) - 1 + t
            ring_copy(feats, fsend, frecv, block, sem, dst).wait_send()
            ring_copy(init, isend, irecv, block, sem, dst).wait_send()

    count = counts[0]
    src = iota((4 * qp, 2 * qp), 0)
    dst_l = iota((4 * qp, 2 * qp), 1)
    for k in range(slots // 2):
        q0, q1 = ids[0, 2 * k], ids[0, 2 * k + 1]
        both = jnp.concatenate([feats[q0 // 2], feats[q1 // 2]], axis=1)
        first = (dst_l < qp) & (src == dst_l + lax.rem(q0, 2) * qp) & (2 * k < count)
        second = (dst_l >= qp) & (src == dst_l + (1 + lax.rem(q1, 2)) * qp) & (2 * k + 1 < count)
        pick = jnp.where(first | second, 1.0, 0.0).astype(bf16)
        chosen[:, k * 2 * qp : (k + 1) * 2 * qp] = jnp.dot(
            both, pick, preferred_element_type=f32).astype(bf16)

    chunk = 128

    def strengths(t, _):
        m = t // (nbi // chunk)
        r = pl.ds(pl.multiple_of(lax.rem(t, nbi // chunk) * chunk, chunk), chunk)
        field = jnp.dot(amp[m, r, :], chosen[...], preferred_element_type=f32)
        table[m, r, :] = (field * field).astype(bf16)
        return 0

    lax.fori_loop(0, modes * nbi // chunk, strengths, 0)

    heads = init[0, 2:3, :]
    for x in range(1, n):
        heads = heads + init[x, 2:3, :]
    wide = n * 16
    heads = heads[:, :wide]
    row = iota((16, wide), 0)
    want = jnp.full((16, wide), -1.0, f32)
    for p in range(slots):
        want = jnp.where(row == p, (ids[0, p] + 1).astype(f32), want)
    for q in range(2):
        want = jnp.where(row == slots + q, (2 * me + q + 1).astype(f32), want)
    onehot[...] = jnp.where(want == heads, 1.0, 0.0).astype(bf16)

    nbase[...] = jnp.zeros_like(nbase)
    for p in range(slots):
        q = ids[0, p]
        two = init[q // 2]
        nbase[p : p + 1, :] = jnp.where(lax.rem(q, 2) == 0, two[0:1, :nmj], two[1:2, :nmj])
    for q in range(2):
        nbase[slots + q : slots + q + 1, :] = init[me, q : q + 1, :nmj]
    rows_s[...] = nbase[...]
    nk1[...] = jnp.zeros_like(nk1)
    fbase[...] = init[me, 3:4, :nbi]
    fnow[...] = init[me, 3:4, :nbi]
    fk1[...] = jnp.zeros_like(fk1)
    before = lax.rem(me + n - 1, n)
    after = lax.rem(me + 1, n)
    rims[0] = jnp.broadcast_to(init[before, 3:4, :nbi], (8, nbi))

    lane = iota((1, nbi), 1)
    drift = jnp.zeros((1, nbi), f32)
    for b in range(bands):
        drift = jnp.where(lane // kp == b, speed[b], drift)
    half_lane = iota((1, 2 * qp), 1) < qp

    def send_msg(e, k):
        dst = lax.rem(me + k, n)
        return pltpu.make_async_remote_copy(
            src_ref=msgs.at[e, me], dst_ref=msgs.at[e, me],
            send_sem=msend.at[e, k], recv_sem=mrecv.at[e, me],
            device_id={"kel": dst}, device_id_type=MESH)

    def take_msg(e, k):
        src_d = lax.rem(me + n - k, n)
        return pltpu.make_async_remote_copy(
            src_ref=msgs.at[e, src_d], dst_ref=msgs.at[e, src_d],
            send_sem=msend.at[e, k], recv_sem=mrecv.at[e, src_d],
            device_id={"kel": src_d}, device_id_type=MESH)

    def rim_copy(e):
        return pltpu.make_async_remote_copy(
            src_ref=rims.at[2 * STEPS + 1 + e], dst_ref=rims.at[e + 1],
            send_sem=rsend.at[e], recv_sem=rrecv.at[e],
            device_id={"kel": after}, device_id_type=MESH)

    def split(x):
        hi = x.astype(bf16).astype(f32)
        return hi, x - hi

    def triple(hi, lo, shape):
        r = iota(shape, 0)
        return jnp.where(r == 0, hi, jnp.where(r == 1, lo, jnp.where(r == 2, 1.0, 0.0))).astype(bf16)

    def evaluate(e, _):
        even = lax.rem(e, 2) == 0
        for mm in range(modes // 2):
            here = rows_s[:, 2 * mm * qp : 2 * (mm + 1) * qp]
            turn = pltpu.roll(here, qp, 1)
            for k in range(slots // 2):
                cols = slice(2 * k * qp, 2 * (k + 1) * qp)
                lanes_s[2 * mm : 2 * mm + 1, cols] = jnp.where(
                    half_lane, here[2 * k : 2 * k + 1], turn[2 * k + 1 : 2 * k + 2])
                lanes_s[2 * mm + 1 : 2 * mm + 2, cols] = jnp.where(
                    half_lane, turn[2 * k : 2 * k + 1], here[2 * k + 1 : 2 * k + 2])
        occ = fnow[...]
        fhi, flo = split(occ)
        fmat = triple(fhi, flo, (8, nbi))
        low = jnp.zeros((8, nbi), f32)
        for m in range(modes):
            tab = table[m]
            tow = jnp.dot(fmat, tab, preferred_element_type=f32)
            toward_s[m : m + 1, :] = tow[0:1] + tow[1:2]
            plain_s[m : m + 1, :] = tow[2:3]
            nhi, nlo = split(lanes_s[m : m + 1, :])
            low = low + lax.dot_general(
                triple(nhi, nlo, (8, npj)), tab, (((1,), (1,)), ((), ())),
                preferred_element_type=f32)
        nl = lanes_s[0:modes, :]
        gained = (1.0 + 2.0 * nl) * toward_s[0:modes, :] - nl * plain_s[0:modes, :]
        for k in range(slots // 2):
            here = gained[:, 2 * k * qp : 2 * (k + 1) * qp]
            turn = pltpu.roll(here, qp, 1)
            for mm in range(modes // 2):
                cols = slice(2 * mm * qp, 2 * (mm + 1) * qp)
                rows_s[2 * k : 2 * k + 1, cols] = jnp.where(
                    half_lane, here[2 * mm : 2 * mm + 1], turn[2 * mm + 1 : 2 * mm + 2])
                rows_s[2 * k + 1 : 2 * k + 2, cols] = jnp.where(
                    half_lane, turn[2 * mm : 2 * mm + 1], here[2 * mm + 1 : 2 * mm + 2])
        live = iota((16, nmj), 0) < slots
        msgs[e, me] = jnp.where(live, rows_s[...], 0.0).astype(bf16)

        def go(k, _):
            send_msg(e, k).start()
            return 0

        lax.fori_loop(1, n, go, 0)

        lower = low[0:1] + low[1:2]
        loss = occ * (low[2:3] + 2.0 * lower) - lower
        ke = -loss / (slots * modes * qp) - drift * (occ - rims[e, 0:1, :])
        nextf = fbase[...] + HALF * (jnp.where(even, ke, fk1[...]) + ke)
        fk1[...] = ke
        fbase[...] = jnp.where(even, fbase[...], nextf)
        fnow[...] = nextf
        rims[2 * STEPS + 1 + e] = jnp.broadcast_to(nextf, (8, nbi))
        rim_copy(e).start()

        def come(k, _):
            take_msg(e, k).wait_recv()
            return 0

        lax.fori_loop(1, n, come, 0)
        every = msgs[e].reshape(n * 16, nmj)
        kn = jnp.dot(onehot[...], every, preferred_element_type=f32) / (slots * bands * kp)
        nextn = nbase[...] + HALF * (jnp.where(even, kn, nk1[...]) + kn)
        nk1[...] = kn
        nbase[...] = jnp.where(even, nbase[...], nextn)
        rows_s[...] = nextn
        rim_copy(e).wait_recv()
        return 0

    lax.fori_loop(0, 2 * STEPS, evaluate, 0)

    for b in range(bands):
        elec_out[0, b : b + 1, :] = fnow[:, b * kp : (b + 1) * kp]
    for q in range(2):
        for m in range(modes):
            phon_out[q, m : m + 1, :] = rows_s[slots + q : slots + q + 1, m * qp : (m + 1) * qp]

    def settle(e, _):
        def gone(k, _):
            send_msg(e, k).wait_send()
            return 0

        lax.fori_loop(1, n, gone, 0)
        rim_copy(e).wait_send()
        return 0

    lax.fori_loop(0, 2 * STEPS, settle, 0)


def body(n, electrons, phonons, elec_wannier, phon_wannier, coupling, pair_blocks, pair_counts, drift_speed):
    _, bands, kp = electrons.shape
    _, modes, qp = phonons.shape
    slots = pair_blocks.shape[1]
    ws = elec_wannier.shape[1]
    nbi, npj, nmj = bands * kp, slots * qp, modes * qp
    width = max(nbi, n * 16, nmj)
    evals = 2 * STEPS
    vmem = pl.BlockSpec(memory_space=pltpu.VMEM)
    smem = pl.BlockSpec(memory_space=pltpu.SMEM)
    dma = pltpu.SemaphoreType.DMA
    return pl.pallas_call(
        functools.partial(kernel, n, bands, modes, kp, qp, slots, ws),
        out_shape=(
            jax.ShapeDtypeStruct(electrons.shape, f32),
            jax.ShapeDtypeStruct(phonons.shape, f32),
        ),
        in_specs=[vmem, vmem, vmem, vmem, pl.BlockSpec(memory_space=pl.ANY), smem, smem, smem],
        out_specs=(vmem, vmem),
        scratch_shapes=[
            pltpu.VMEM(coupling.shape, bf16),
            pltpu.VMEM((modes, nbi, ws), bf16),
            pltpu.VMEM((modes, nbi, npj), bf16),
            pltpu.VMEM((n, ws, 2 * qp), bf16),
            pltpu.VMEM((n, 8, width), f32),
            pltpu.VMEM((ws, npj), bf16),
            pltpu.VMEM((evals, n, 16, nmj), bf16),
            pltpu.VMEM((2 * evals + 1, 8, nbi), f32),
            pltpu.VMEM((16, nmj), f32),
            pltpu.VMEM((8, npj), f32),
            pltpu.VMEM((8, npj), f32),
            pltpu.VMEM((8, npj), f32),
            pltpu.VMEM((16, nmj), f32),
            pltpu.VMEM((16, nmj), f32),
            pltpu.VMEM((1, nbi), f32),
            pltpu.VMEM((1, nbi), f32),
            pltpu.VMEM((1, nbi), f32),
            pltpu.VMEM((16, n * 16), bf16),
            dma((bands,)),
            dma((n,)), dma((n,)), dma((n,)), dma((n,)),
            dma((evals, n)), dma((evals, n)),
            dma((evals,)), dma((evals,)),
        ],
        compiler_params=pltpu.CompilerParams(
            collective_id=0, has_side_effects=True, vmem_limit_bytes=40 * 2**20),
    )(electrons, phonons, elec_wannier, phon_wannier, coupling, pair_blocks, pair_counts, drift_speed)


def solution(mesh):
    rows3 = P(("groups", "kel"), None, None)
    placed = (rows3, rows3, rows3, rows3, P(), P(("groups", "kel"), None), P(("groups", "kel")), P("groups"))
    return jax.shard_map(
        functools.partial(body, mesh.shape["kel"]),
        mesh=mesh, in_specs=placed, out_specs=(rows3, rows3), check_vma=False)
```

```python
import functools
import jax
import jax.numpy as jnp
from jax import lax
from jax.experimental import pallas as pl
from jax.experimental.pallas import tpu as pltpu
from jax.sharding import PartitionSpec as P

STEPS = 2
HALF = 0.25
FULL = 0.5
MESH = pl.DeviceIdType.MESH
f32 = jnp.float32
bf16 = jnp.bfloat16


def iota(shape, dim):
    return lax.broadcasted_iota(jnp.int32, shape, dim)


def kernel(
    n, bands, modes, kp, qp, slots, ws,
    elec, phon, ew, pw, coup, ids_h, counts_h, speed_h,
    elec_out, phon_out,
    coup_v, amp, table, feats, init, chosen, msgs, rims,
    rows_s, trow, prow, lanes_s, plain_s, toward_s, nbase, nk1, fbase, fk1, fnow, onehot,
    ewt, elec_v, phon_v, ids, counts, speed,
    csem, asem, fsend, frecv, isend, irecv, msend, mrecv, rsend, rrecv,
):
    me = lax.axis_index("kel")
    nbi = bands * kp
    npj = slots * qp
    nmj = modes * qp
    width = init.shape[2]
    bits = n.bit_length() - 1
    chips = n // 2
    mate = me + 1 - 2 * lax.rem(me, 2)

    small = [
        pltpu.make_async_copy(x, y, asem.at[i])
        for i, (x, y) in enumerate((
            (ids_h, ids), (phon, phon_v), (elec, elec_v), (pw, feats.at[pl.ds(2 * me, 2)]),
            (ew, ewt), (counts_h, counts), (speed_h, speed)))
    ]
    for copy in small:
        copy.start()

    def load_coupling(b):
        span = pl.ds(b * modes, modes)
        return pltpu.make_async_copy(coup.at[span], coup_v.at[span], csem.at[b])

    for b in range(bands):
        load_coupling(b).start()

    barrier = pltpu.get_barrier_semaphore()

    def partner(bit):
        step = 1 << bit
        return me + step * (1 - 2 * lax.rem(me // step, 2))

    for bit in range(bits):
        pl.semaphore_signal(
            barrier, inc=1, device_id={"kel": partner(bit)}, device_id_type=MESH)

    for copy in small:
        copy.wait()
    own = jnp.zeros((4, width), f32)
    rows = iota((4, width), 0)
    lanes = iota((4, width), 1)
    for p in range(slots):
        own = jnp.where((rows == 2) & (lanes == me * 16 + p), (ids[0, p] + 1).astype(f32), own)
    init[me] = own
    for q in range(2):
        for m in range(modes):
            init[me, q : q + 1, m * qp : (m + 1) * qp] = phon_v[m, q : q + 1, :]
    for b in range(bands):
        init[me, 3:4, b * kp : (b + 1) * kp] = elec_v[0, b : b + 1, :]
    pl.semaphore_wait(barrier, bits)

    def tree_copies(flips, bit):
        block = me
        for other in flips:
            block = block + partner(other) - me
        return [
            pltpu.make_async_remote_copy(
                src_ref=ref.at[where], dst_ref=ref.at[where],
                send_sem=ssem.at[sum(1 << x for x in flips) + (1 << bit)], recv_sem=rsem.at[block],
                device_id={"kel": partner(bit)}, device_id_type=MESH)
            for ref, where, ssem, rsem in (
                (feats, pl.ds(2 * block, 2), fsend, frecv), (init, block, isend, irecv))
        ]

    subsets = [[bit for bit in range(bits) if v >> bit & 1] for v in range(n)]
    subsets.sort(key=lambda flips: (len(flips), min(flips + [bits]) == 0, -sum(1 << x for x in flips)))

    def pass_on(flips):
        for bit in range(min(flips + [bits]) - 1, -1, -1):
            for copy in tree_copies(flips, bit):
                copy.start()

    pass_on([])

    def amps(b, _):
        load_coupling(b).wait()
        for m in range(modes):
            a = jnp.dot(ewt[0], coup_v[b * modes + m], preferred_element_type=f32)
            amp[m, pl.ds(pl.multiple_of(b * kp, kp), kp), :] = a.astype(bf16)
        return 0

    done = 0
    for flips in subsets[1:]:
        if done < bands:
            lax.fori_loop(done, min(bands, done + 2), amps, 0)
            done += 2
        for copy in tree_copies(flips, min(flips)):
            copy.wait_recv()
        pass_on(flips)
    if done < bands:
        lax.fori_loop(done, bands, amps, 0)

    count = counts[0]
    for k in range(slots // 2):
        pair = [
            jnp.where(2 * k + i < count, feats[ids[0, 2 * k + i]].astype(f32), 0.0) for i in range(2)
        ]
        chosen[:, k * 2 * qp : (k + 1) * 2 * qp] = jnp.transpose(
            jnp.concatenate(pair, axis=0)).astype(bf16)

    chunk = nbi

    def strengths(t, _):
        m = t // (nbi // chunk)
        r = pl.ds(pl.multiple_of(lax.rem(t, nbi // chunk) * chunk, chunk), chunk)
        field = jnp.dot(amp[m, r, :], chosen[...], preferred_element_type=f32)
        table[m, r, :] = (field * field).astype(bf16)
        return 0

    lax.fori_loop(0, modes * nbi // chunk, strengths, 0)

    heads = init[0, 2:3, :]
    for x in range(1, n):
        heads = heads + init[x, 2:3, :]
    wide = n * 16
    heads = heads[:, :wide]
    row = iota((16, wide), 0)
    want = jnp.full((16, wide), -1.0, f32)
    for p in range(slots):
        want = jnp.where(row == p, (ids[0, p] + 1).astype(f32), want)
    for q in range(2):
        want = jnp.where(row == slots + q, (2 * me + q + 1).astype(f32), want)
    onehot[...] = jnp.where(want == heads, 1.0, 0.0).astype(bf16)

    nbase[...] = jnp.zeros_like(nbase)
    for p in range(slots):
        q = ids[0, p]
        two = init[q // 2]
        nbase[p : p + 1, :] = jnp.where(lax.rem(q, 2) == 0, two[0:1, :nmj], two[1:2, :nmj])
    for q in range(2):
        nbase[slots + q : slots + q + 1, :] = init[me, q : q + 1, :nmj]
    rows_s[...] = nbase[...]
    nk1[...] = jnp.zeros_like(nk1)
    fbase[...] = init[me, 3:4, :nbi]
    fnow[...] = init[me, 3:4, :nbi]
    fk1[...] = jnp.zeros_like(fk1)
    before = lax.rem(me + n - 1, n)
    after = lax.rem(me + 1, n)
    rims[0] = init[before, 3:4, :nbi]

    lane = iota((1, nbi), 1)
    drift = jnp.zeros((1, nbi), f32)
    for b in range(bands):
        drift = jnp.where(lane // kp == b, speed[b], drift)
    half_lane = iota((1, 2 * qp), 1) < qp

    def msg_copy(e, block, sem, dst):
        return pltpu.make_async_remote_copy(
            src_ref=msgs.at[e, block], dst_ref=msgs.at[e, block],
            send_sem=msend.at[e, sem], recv_sem=mrecv.at[e, block],
            device_id={"kel": dst}, device_id_type=MESH)

    def spread(e, k):
        return msg_copy(e, me, k, lax.rem(me + 2 * k, n))

    def arrive(e, k):
        return msg_copy(e, lax.rem(me + n - 2 * k, n), k, mate)

    def forward(e, k):
        return msg_copy(e, lax.rem(me + n - 2 * k, n), chips + k, mate)

    def relayed(e, k):
        return msg_copy(e, lax.rem(mate + n - 2 * k, n), k, mate)

    def rim_copy(e):
        return pltpu.make_async_remote_copy(
            src_ref=rims.at[2 * STEPS + e], dst_ref=rims.at[e + 1],
            send_sem=rsend.at[e], recv_sem=rrecv.at[e],
            device_id={"kel": after}, device_id_type=MESH)

    def split(x):
        hi = x.astype(bf16).astype(f32)
        return hi, x - hi

    def triple(hi, lo, shape):
        r = iota(shape, 0)
        return jnp.where(r == 0, hi, jnp.where(r == 1, lo, jnp.where(r == 2, 1.0, 0.0))).astype(bf16)

    def to_rows(src_ref, dst_ref):
        for k in range(slots // 2):
            here = src_ref[:, 2 * k * qp : 2 * (k + 1) * qp]
            turn = pltpu.roll(here, qp, 1)
            for mm in range(modes // 2):
                cols = slice(2 * mm * qp, 2 * (mm + 1) * qp)
                dst_ref[2 * k : 2 * k + 1, cols] = jnp.where(
                    half_lane, here[2 * mm : 2 * mm + 1], turn[2 * mm + 1 : 2 * mm + 2])
                dst_ref[2 * k + 1 : 2 * k + 2, cols] = jnp.where(
                    half_lane, turn[2 * mm : 2 * mm + 1], here[2 * mm + 1 : 2 * mm + 2])

    def to_lanes(src_ref, dst_ref):
        for mm in range(modes // 2):
            here = src_ref[:, 2 * mm * qp : 2 * (mm + 1) * qp]
            turn = pltpu.roll(here, qp, 1)
            for k in range(slots // 2):
                cols = slice(2 * k * qp, 2 * (k + 1) * qp)
                dst_ref[2 * mm : 2 * mm + 1, cols] = jnp.where(
                    half_lane, here[2 * k : 2 * k + 1], turn[2 * k + 1 : 2 * k + 2])
                dst_ref[2 * mm + 1 : 2 * mm + 2, cols] = jnp.where(
                    half_lane, turn[2 * k : 2 * k + 1], here[2 * k + 1 : 2 * k + 2])

    def toward_of(occ):
        fhi, flo = split(occ)
        fmat = triple(fhi, flo, (8, nbi))
        for m in range(modes):
            tow = jnp.dot(fmat, table[m], preferred_element_type=f32)
            toward_s[m : m + 1, :] = tow[0:1] + tow[1:2]
            plain_s[m : m + 1, :] = tow[2:3]
        to_rows(toward_s, trow)

    trow[...] = jnp.zeros_like(trow)
    prow[...] = jnp.zeros_like(prow)
    toward_of(fnow[...])
    to_rows(plain_s, prow)
    evals = 2 * STEPS

    def evaluate(e, _):
        even = lax.rem(e, 2) == 0
        occ_n = rows_s[...]
        gained = (1.0 + 2.0 * occ_n) * trow[...] - occ_n * prow[...]
        msgs[e, me] = gained.astype(bf16)
        for k in range(1, chips):
            spread(e, k).start()
        msg_copy(e, me, 0, mate).start()

        to_lanes(rows_s, lanes_s)
        low = jnp.zeros((8, nbi), f32)
        for m in range(modes):
            nhi, nlo = split(lanes_s[m : m + 1, :])
            low = low + lax.dot_general(
                triple(nhi, nlo, (8, npj)), table[m], (((1,), (1,)), ((), ())),
                preferred_element_type=f32)
        lower = low[0:1] + low[1:2]
        occ = fnow[...]
        loss = occ * (low[2:3] + 2.0 * lower) - lower

        @pl.when(e > 0)
        def _():
            rim_copy(e - 1).wait_recv()

        ke = -loss / (slots * modes * qp) - drift * (occ - rims[e])
        nextf = fbase[...] + HALF * (jnp.where(even, ke, fk1[...]) + ke)
        fk1[...] = ke
        fbase[...] = jnp.where(even, fbase[...], nextf)
        fnow[...] = nextf

        @pl.when(e < evals - 1)
        def _():
            rims[evals + e] = nextf
            rim_copy(e).start()
            toward_of(nextf)

        for k in range(1, chips):
            arrive(e, k).wait_recv()
            forward(e, k).start()
        for k in range(chips):
            relayed(e, k).wait_recv()
        every = msgs[e].reshape(n * 16, nmj)
        kn = jnp.dot(onehot[...], every, preferred_element_type=f32) / (slots * bands * kp)
        nextn = nbase[...] + HALF * (jnp.where(even, kn, nk1[...]) + kn)
        nk1[...] = kn
        nbase[...] = jnp.where(even, nbase[...], nextn)
        rows_s[...] = nextn
        return 0

    lax.fori_loop(0, evals, evaluate, 0)

    for b in range(bands):
        elec_out[0, b : b + 1, :] = fnow[:, b * kp : (b + 1) * kp]
    for q in range(2):
        for m in range(modes):
            phon_out[m, q : q + 1, :] = rows_s[slots + q : slots + q + 1, m * qp : (m + 1) * qp]

    def settle(e, _):
        msg_copy(e, me, 0, mate).wait_send()
        for k in range(1, chips):
            spread(e, k).wait_send()
            forward(e, k).wait_send()
        return 0

    lax.fori_loop(0, evals, settle, 0)
    for e in range(evals - 1):
        rim_copy(e).wait_send()
    for flips in subsets:
        for bit in range(min(flips + [bits])):
            for copy in tree_copies(flips, bit):
                copy.wait_send()


def body(n, electrons, phonons, elec_wannier, phon_wannier, coupling, pair_blocks, pair_counts, drift_speed):
    _, bands, kp = electrons.shape
    _, modes, qp = phonons.shape
    slots = pair_blocks.shape[1]
    ws = elec_wannier.shape[1]
    nbi, npj, nmj = bands * kp, slots * qp, modes * qp
    width = max(nbi, n * 16, nmj)
    evals = 2 * STEPS
    vmem = pl.BlockSpec(memory_space=pltpu.VMEM)
    dma = pltpu.SemaphoreType.DMA
    elec_o, phon_o = pl.pallas_call(
        functools.partial(kernel, n, bands, modes, kp, qp, slots, ws),
        out_shape=(
            jax.ShapeDtypeStruct(electrons.shape, f32),
            jax.ShapeDtypeStruct((modes, 2, qp), f32),
        ),
        in_specs=[pl.BlockSpec(memory_space=pltpu.HBM)] * 8,
        out_specs=(vmem, vmem),
        scratch_shapes=[
            pltpu.VMEM(coupling.shape, bf16),
            pltpu.VMEM((modes, nbi, ws), bf16),
            pltpu.VMEM((modes, nbi, npj), bf16),
            pltpu.VMEM((2 * n, qp, ws), bf16),
            pltpu.VMEM((n, 4, width), f32),
            pltpu.VMEM((ws, npj), bf16),
            pltpu.VMEM((evals, n, 16, nmj), bf16),
            pltpu.VMEM((2 * evals - 1, 1, nbi), f32),
            pltpu.VMEM((16, nmj), f32),
            pltpu.VMEM((16, nmj), f32),
            pltpu.VMEM((16, nmj), f32),
            pltpu.VMEM((8, npj), f32),
            pltpu.VMEM((8, npj), f32),
            pltpu.VMEM((8, npj), f32),
            pltpu.VMEM((16, nmj), f32),
            pltpu.VMEM((16, nmj), f32),
            pltpu.VMEM((1, nbi), f32),
            pltpu.VMEM((1, nbi), f32),
            pltpu.VMEM((1, nbi), f32),
            pltpu.VMEM((16, n * 16), bf16),
            pltpu.VMEM((1, kp, ws), bf16),
            pltpu.VMEM(electrons.shape, f32),
            pltpu.VMEM((modes, 2, qp), f32),
            pltpu.SMEM(pair_blocks.shape, jnp.int32),
            pltpu.SMEM(pair_counts.shape, jnp.int32),
            pltpu.SMEM(drift_speed.shape, f32),
            dma((bands,)), dma((7,)),
            dma((n,)), dma((n,)), dma((n,)), dma((n,)),
            dma((evals, n)), dma((evals, n)),
            dma((evals,)), dma((evals,)),
        ],
        compiler_params=pltpu.CompilerParams(
            collective_id=0, has_side_effects=True, vmem_limit_bytes=60 * 2**20),
    )(
        electrons, jnp.transpose(phonons, (1, 0, 2)), jnp.swapaxes(elec_wannier, 1, 2),
        jnp.swapaxes(phon_wannier, 1, 2), coupling, pair_blocks, pair_counts, drift_speed)
    return elec_o, jnp.transpose(phon_o, (1, 0, 2))


def solution(mesh):
    rows3 = P(("groups", "kel"), None, None)
    placed = (rows3, rows3, rows3, rows3, P(), P(("groups", "kel"), None), P(("groups", "kel")), P("groups"))
    return jax.shard_map(
        functools.partial(body, mesh.shape["kel"]),
        mesh=mesh, in_specs=placed, out_specs=(rows3, rows3), check_vma=False)
```
